32 devices in a mesh: row: 8 (over z, core), col: 4 (over y, x).
Axes of the slice: x: 2, y: 2, z: 4, core: 2. Of those that a mesh axis runs over, the one named last changes fastest.
Arguments:
- matrix: float32 [4, 1024, 8, 512], P(None, 'row', None, 'col'), may hold values from 0 to 11, as said below
Outputs:
- factored: float32 [4, 1024, 8, 512], P(None, 'row', None, 'col')
The draws below stay inside these ranges and needn't reach their ends.
Inputs may be any that keep to these rules, and one draw needn't show every extreme that they name: matrix is symmetric and positive definite.
All inputs are finite; a program needn't handle non-finite values.
Results may differ from the reference program's by a relative error of at most 0.0003.
Values sent between devices are 32-bit elements; how exact they have to be, the bound alone decides.
A program may use at most 64 MiB of HBM per device.

```python
import jax
import jax.numpy as jnp
from jax import lax

B = 128
TR = 4
PANELS = 2
TC = 8
ORDER = 4096


def kernel_build(points, amplitude, lengthscale, jitter):
    total = jnp.zeros((points.shape[0], points.shape[0]), jnp.float32)
    for feature in range(8):
        column = points[:, feature] / lengthscale
        differ = column[:, None] - column[None, :]
        total = total + differ * differ
    kernel = amplitude[:, None] * amplitude[None, :] * jnp.exp(-0.5 * total)
    return kernel + jitter * jnp.eye(points.shape[0], dtype=jnp.float32)


def draw_matrix(key, part):
    key = jax.random.fold_in(key, 7)
    key_points, key_amp = jax.random.split(key)
    amplitude = jnp.exp(jax.random.uniform(key_amp, (ORDER,), jnp.float32, -1.15, 1.15))
    points = jax.random.normal(key_points, (ORDER, 8), jnp.float32)
    kernel = kernel_build(points, amplitude, 2.0, 0.5)
    return kernel.reshape(TR, ORDER // TR, TC, ORDER // TC)


def setup_inputs(seed: int = 0) -> dict:
    seeds = jax.random.split(jax.random.key(seed), 2)
    return {
        "matrix": draw_matrix(jax.random.fold_in(seeds[1], 71), 0),
    }


def reference(matrix):
    order = matrix.shape[0] * matrix.shape[1]
    whole = matrix.reshape(order, order)
    for panel in range(PANELS):
        start = panel * B
        end = start + B
        tile = jnp.linalg.cholesky(whole[start:end, start:end])
        below = lax.linalg.triangular_solve(tile, whole[end:, start:end], left_side=False, lower=True, transpose_a=True)
        update = jnp.dot(below, below.T, precision=lax.Precision.HIGHEST)
        whole = whole.at[end:, end:].add(-update)
        column = jnp.concatenate([jnp.zeros((start, B), jnp.float32), tile, below], 0)
        whole = whole.at[:, start:end].set(column)
    return jnp.tril(whole).reshape(matrix.shape)
```

```python
import functools

import jax
import jax.numpy as jnp
from jax import lax
from jax.experimental import pallas as pl
from jax.experimental.pallas import tpu as pltpu
from jax.sharding import PartitionSpec as P

MESH = pl.DeviceIdType.MESH
HIGHEST = lax.Precision.HIGHEST
CHUNKS = 4


def dot(a, b, dims):
    return lax.dot_general(
        a, b, (dims, ((), ())), precision=HIGHEST, preferred_element_type=jnp.float32
    )


NN = ((1,), (0,))
NT = ((1,), (1,))
TN = ((0,), (0,))


def invert_factor(aug):
    n = aug.shape[0]
    rows = lax.broadcasted_iota(jnp.int32, (n, n), 0)
    lanes = lax.broadcasted_iota(jnp.int32, (n, n), 1)
    aug[:, n:] = jnp.where(rows == lanes, 1.0, 0.0)
    sub = lax.broadcasted_iota(jnp.int32, (8, n), 0)
    lane = lax.broadcasted_iota(jnp.int32, (8, n), 1)

    def block(b, carry):
        base = pl.multiple_of(b * 8, 8)
        left = aug[pl.ds(base, 8), :n]
        right = aug[pl.ds(base, 8), n:]
        diag = pltpu.roll(left, n - base, 1)
        cols = [jnp.broadcast_to(diag[:, k : k + 1], (8, n)) for k in range(8)]
        scale = jnp.zeros((8, n), jnp.float32)
        for k in range(8):
            inverse = lax.rsqrt(jnp.broadcast_to(cols[k][k : k + 1], (8, n)))
            scale = jnp.where(sub == k, inverse, scale)
            if k == 7:
                break
            factor = cols[k] * inverse
            below = jnp.where(sub > k, factor, 0.0)
            for j in range(k + 1, 8):
                cols[j] = cols[j] - factor * jnp.broadcast_to(factor[j : j + 1], (8, n))
            left = left - below * (jnp.broadcast_to(left[k : k + 1], (8, n)) * inverse)
            right = right - below * (jnp.broadcast_to(right[k : k + 1], (8, n)) * inverse)
        left = left * scale
        right = right * scale
        later = jnp.where(lane >= base + 8, left, 0.0)
        aug[...] -= dot(later, jnp.concatenate([left, right], 1), TN)
        aug[pl.ds(base, 8), n:] = right
        return carry

    lax.fori_loop(0, n // 8, block, 0)


def kernel(
    rows_n, cols_n, m_ref, o_ref, row_p, col_p, first, second, corner, aug, x_s, r_s, y_s,
    send_p, recv_p, send_c, recv_c, send_w, recv_w, send_t, recv_t,
):
    r = lax.axis_index("row")
    c = lax.axis_index("col")
    tiles_r, height, width = m_ref.shape
    tiles_c = height // width
    parity = lax.rem(r, 2)
    sibling = r + 1 - 2 * parity
    root = jnp.logical_and(r == 0, c == 0)
    corner_owner = jnp.logical_and(r == 1, c == 1)

    barrier = pltpu.get_barrier_semaphore()
    for step in range(1, cols_n):
        pl.semaphore_signal(
            barrier, inc=1, device_id=(r, lax.rem(c + step, cols_n)), device_id_type=MESH
        )
    for step in range(1, rows_n):
        pl.semaphore_signal(
            barrier, inc=1, device_id=(lax.rem(r + step, rows_n), c), device_id_type=MESH
        )

    @pl.when(jnp.logical_or(root, corner_owner))
    def _():
        pl.semaphore_signal(barrier, inc=1, device_id=(1 - r, 1 - c), device_id_type=MESH)

    @pl.when(c < 2)
    def _():
        for t in range(tiles_r):
            row_p[c, t] = m_ref[t, pl.ds(0, width, stride=tiles_c), :]

    @pl.when(r < 2)
    def _():
        col_p[parity] = m_ref[0]

    on_diagonal = jnp.logical_or(root, corner_owner)

    @pl.when(on_diagonal)
    def _():
        pl.semaphore_wait(barrier, rows_n + cols_n - 1)

    @pl.when(jnp.logical_not(on_diagonal))
    def _():
        pl.semaphore_wait(barrier, rows_n + cols_n - 2)

    def send(src, dst, send_sem, recv_sem, device):
        return pltpu.make_async_remote_copy(
            src_ref=src, dst_ref=dst, send_sem=send_sem, recv_sem=recv_sem,
            device_id=device, device_id_type=MESH,
        )

    def corner_copy():
        return send(row_p.at[1, 0], corner, send_t, recv_t, (0, 0))

    def panel_copy(step):
        return send(
            row_p.at[c], row_p.at[c], send_p.at[step - 1], recv_p.at[c],
            (r, lax.rem(c + step, cols_n)),
        )

    chunk = height // CHUNKS

    def chain_copy(which, k, panel):
        part = col_p.at[panel, pl.ds(k * chunk, chunk)]
        target = (sibling, c) if which == 0 else (r + 2, c)
        return send(part, part, send_c.at[which, k], recv_c.at[panel, k], target)

    def spread_copy(phase, step, device):
        buffer = (first, second)[phase]
        return send(buffer, buffer, send_w.at[phase, step], recv_w.at[phase], device)

    pairs = rows_n // 2

    def spread(phase, act):
        @pl.when(root)
        def _():
            for step in range(1, cols_n):
                act(spread_copy(phase, step - 1, (0, step)))

        @pl.when(r == 0)
        def _():
            for step in range(1, pairs):
                act(spread_copy(phase, cols_n - 2 + step, (2 * step, c)))

        @pl.when(parity == 0)
        def _():
            act(spread_copy(phase, cols_n - 2 + pairs, (r + 1, c)))

    def wait_spread(phase):
        @pl.when(jnp.logical_not(root))
        def _():
            spread_copy(phase, 0, (sibling, c)).wait_recv()

    @pl.when(corner_owner)
    def _():
        corner_copy().start()

    @pl.when(c < 2)
    def _():
        for step in range(1, cols_n):
            panel_copy(step).start()

    for k in range(CHUNKS):
        @pl.when(r >= 2)
        def _():
            chain_copy(0, k, parity).wait_recv()

        @pl.when(r + 2 < rows_n)
        def _():
            chain_copy(1, k, parity).start()

        chain_copy(0, k, parity).start()

    def wait_panel(panel):
        @pl.when(c != panel)
        def _():
            send(
                row_p.at[panel], row_p.at[panel], send_p.at[0], recv_p.at[panel], (sibling, c)
            ).wait_recv()

    @pl.when(root)
    def _():
        aug[:, :width] = row_p[0, 0]
        invert_factor(aug)
        first[:width] = aug[:, width:]
        wait_panel(1)
        first[width:] = dot(row_p[1, 0], first[:width], ((0,), (1,)))

    @pl.when(jnp.logical_not(root))
    def _():
        wait_panel(1)

    wait_spread(0)
    spread(0, lambda copy: copy.start())

    @pl.when(root)
    def _():
        corner_copy().wait_recv()
        lower = first[width:]
        aug[:, :width] = corner[...] - dot(lower, lower, NT)
        invert_factor(aug)
        second[...] = aug[:, width:]
        spread(1, lambda copy: copy.start())

    wait_panel(0)
    for k in range(CHUNKS):
        chain_copy(0, k, 1 - parity).wait_recv()

    w0 = first[:width]
    lower = first[width:]
    last = [min(tiles_c, ((t + 1) * rows_n - 1) // cols_n + 1) for t in range(tiles_r)]
    for t in range(tiles_r):
        x0 = dot(row_p[0, t], w0, NT)
        x_s[0, t] = x0
        r_s[t] = row_p[1, t] - dot(x0, lower, NT)
    for s in range(tiles_c):
        part = pl.ds(s, width, stride=tiles_c)
        y0 = dot(w0, col_p[0, part, :], NN)
        y_s[0, s] = y0
        y_s[1, s] = col_p[1, part, :] - dot(lower, y0, NN)
    for t in range(tiles_r):
        for s in range(last[t]):
            part = pl.ds(s, width, stride=tiles_c)
            o_ref[t, part, :] = m_ref[t, part, :] - dot(x_s[0, t], y_s[0, s], NN)

    wait_spread(1)

    @pl.when(jnp.logical_not(root))
    def _():
        spread(1, lambda copy: copy.start())

    w1 = second[...]
    for t in range(tiles_r):
        x_s[1, t] = dot(r_s[t], w1, NT)
    for s in range(tiles_c):
        y_s[1, s] = dot(w1, y_s[1, s], NN)
    down = lax.broadcasted_iota(jnp.int32, (width, width), 0)
    across = lax.broadcasted_iota(jnp.int32, (width, width), 1)
    ahead = down - across
    for t in range(tiles_r):
        for s in range(tiles_c):
            part = pl.ds(s, width, stride=tiles_c)
            if s >= last[t]:
                o_ref[t, part, :] = jnp.zeros((width, width), jnp.float32)
                continue
            value = o_ref[t, part, :] - dot(x_s[1, t], y_s[1, s], NN)
            if s == 0:
                value = jnp.where(c == 0, x_s[0, t], jnp.where(c == 1, x_s[1, t], value))
            offset = ((t * rows_n + r) - (s * cols_n + c)) * width
            o_ref[t, part, :] = jnp.where(ahead + offset >= 0, value, 0.0)

    @pl.when(corner_owner)
    def _():
        corner_copy().wait_send()

    @pl.when(c < 2)
    def _():
        for step in range(1, cols_n):
            panel_copy(step).wait_send()

    for k in range(CHUNKS):
        @pl.when(r + 2 < rows_n)
        def _():
            chain_copy(1, k, parity).wait_send()

        chain_copy(0, k, parity).wait_send()
    for phase in range(2):
        spread(phase, lambda copy: copy.wait_send())


def body(matrix, rows_n, cols_n):
    tiles_r, width, tiles_c, _ = matrix.shape
    height = width * tiles_c
    spreads = cols_n - 1 + rows_n // 2
    f32 = jnp.float32
    out = pl.pallas_call(
        functools.partial(kernel, rows_n, cols_n),
        out_shape=jax.ShapeDtypeStruct((tiles_r, height, width), f32),
        in_specs=[pl.BlockSpec(memory_space=pltpu.VMEM)],
        out_specs=pl.BlockSpec(memory_space=pltpu.VMEM),
        scratch_shapes=[
            pltpu.VMEM((2, tiles_r, width, width), f32),
            pltpu.VMEM((2, height, width), f32),
            pltpu.VMEM((2 * width, width), f32),
            pltpu.VMEM((width, width), f32),
            pltpu.VMEM((width, width), f32),
            pltpu.VMEM((width, 2 * width), f32),
            pltpu.VMEM((2, tiles_r, width, width), f32),
            pltpu.VMEM((tiles_r, width, width), f32),
            pltpu.VMEM((2, tiles_c, width, width), f32),
            pltpu.SemaphoreType.DMA((cols_n - 1,)),
            pltpu.SemaphoreType.DMA((2,)),
            pltpu.SemaphoreType.DMA((2, CHUNKS)),
            pltpu.SemaphoreType.DMA((2, CHUNKS)),
            pltpu.SemaphoreType.DMA((2, spreads)),
            pltpu.SemaphoreType.DMA((2,)),
            pltpu.SemaphoreType.DMA(()),
            pltpu.SemaphoreType.DMA(()),
        ],
        compiler_params=pltpu.CompilerParams(
            collective_id=0, has_side_effects=True, vmem_limit_bytes=32 * 1024 * 1024
        ),
    )(matrix.reshape(tiles_r, height, width))
    return out.reshape(matrix.shape)


def solution(mesh):
    placed = P(None, "row", None, "col")
    return jax.shard_map(
        functools.partial(body, rows_n=mesh.shape["row"], cols_n=mesh.shape["col"]),
        mesh=mesh, in_specs=(placed,), out_specs=placed, check_vma=False,
    )
```

```python
import functools

import jax
import jax.numpy as jnp
from jax import lax
from jax.experimental import pallas as pl
from jax.experimental.pallas import tpu as pltpu
from jax.sharding import PartitionSpec as P

MESH = pl.DeviceIdType.MESH
HIGHEST = lax.Precision.HIGHEST
CHUNKS = 8
GROUPS = 2
PART = 2
HEAD = 2


def dot(a, b, dims):
    return lax.dot_general(
        a, b, (dims, ((), ())), precision=HIGHEST, preferred_element_type=jnp.float32
    )


NN = ((1,), (0,))
NT = ((1,), (1,))
TN = ((0,), (0,))


def split(x):
    high = x.astype(jnp.bfloat16).astype(jnp.float32)
    rest = x - high
    middle = rest.astype(jnp.bfloat16).astype(jnp.float32)
    return high, middle, rest - middle


def outer_product(a, b):
    a0, a1, a2 = split(a)
    b0, b1, b2 = split(b)
    left = jnp.concatenate([a0, a0, a1, a0, a2, a1], 0).astype(jnp.bfloat16)
    right = jnp.concatenate([b0, b1, b0, b2, b0, b1], 0).astype(jnp.bfloat16)
    return lax.dot_general(left, right, (TN, ((), ())), preferred_element_type=jnp.float32)


def identity_beside(aug):
    n = aug.shape[0]
    rows = lax.broadcasted_iota(jnp.int32, (n, n), 0)
    lanes = lax.broadcasted_iota(jnp.int32, (n, n), 1)
    aug[:, n:] = jnp.where(rows == lanes, 1.0, 0.0)


def eliminate(aug, first, last):
    n = aug.shape[0]
    sub = lax.broadcasted_iota(jnp.int32, (8, n), 0)
    lane = lax.broadcasted_iota(jnp.int32, (8 * GROUPS, n), 1)
    block = 8 * GROUPS

    def spread_row(x, i):
        return jnp.broadcast_to(x[i : i + 1], (8, n))

    for b in range(first, last):
        base = b * block
        left = [aug[base + 8 * g : base + 8 * g + 8, :n] for g in range(GROUPS)]
        right = [aug[base + 8 * g : base + 8 * g + 8, n:] for g in range(GROUPS)]
        cols = [
            [jnp.broadcast_to(left[g][:, base + k : base + k + 1], (8, n)) for k in range(8 * g + 8)]
            for g in range(GROUPS)
        ]
        scale = [jnp.zeros((8, n), jnp.float32) for _ in range(GROUPS)]
        for k in range(block):
            own, row = divmod(k, 8)
            inverse = lax.rsqrt(spread_row(cols[own][k], row))
            scale[own] = jnp.where(sub == row, inverse, scale[own])
            if k == block - 1:
                break
            factor = {g: cols[g][k] * inverse for g in range(own, GROUPS)}
            row_left = spread_row(left[own], row) * inverse
            row_right = spread_row(right[own], row) * inverse
            pivots = {j: spread_row(factor[j // 8], j % 8) for j in range(k + 1, block)}
            for g in range(own, GROUPS):
                if g == own and row == 7:
                    continue
                for j in range(k + 1, 8 * g + 8):
                    cols[g][j] = cols[g][j] - factor[g] * pivots[j]
                below = jnp.where(sub > row, factor[g], 0.0) if g == own else factor[g]
                left[g] = left[g] - below * row_left
                right[g] = right[g] - below * row_right
        done_right = jnp.concatenate([right[g] * scale[g] for g in range(GROUPS)], 0)
        if base + block < n:
            done_left = jnp.concatenate([left[g] * scale[g] for g in range(GROUPS)], 0)
            later = jnp.where(lane >= base + block, done_left, 0.0)
            change = outer_product(later, jnp.concatenate([done_left, done_right], 1))
            aug[base + block :] -= change[base + block :]
        aug[base : base + block, n:] = done_right


def kernel(
    rows_n, cols_n, m_ref, o_ref, row_p, col_p, first, second, corner, aug, x_s, r_s, y_s,
    send_p, recv_p, send_c, recv_c, send_w, recv_w, send_t, recv_t,
):
    r = lax.axis_index("row")
    c = lax.axis_index("col")
    tiles_r, height, width = m_ref.shape
    tiles_c = height // width
    parity = lax.rem(r, 2)
    sibling = r + 1 - 2 * parity
    root = jnp.logical_and(r == 0, c == 0)
    corner_owner = jnp.logical_and(r == 1, c == 1)

    barrier = pltpu.get_barrier_semaphore()
    for step in range(1, cols_n):
        pl.semaphore_signal(
            barrier, inc=1, device_id=(r, lax.rem(c + step, cols_n)), device_id_type=MESH
        )
    for step in range(1, rows_n):
        pl.semaphore_signal(
            barrier, inc=1, device_id=(lax.rem(r + step, rows_n), c), device_id_type=MESH
        )

    @pl.when(jnp.logical_or(root, corner_owner))
    def _():
        pl.semaphore_signal(barrier, inc=1, device_id=(1 - r, 1 - c), device_id_type=MESH)

    @pl.when(c < 2)
    def _():
        for t in range(tiles_r):
            row_p[c, t] = m_ref[t, pl.ds(0, width, stride=tiles_c), :]

    @pl.when(r < 2)
    def _():
        col_p[parity] = m_ref[0]

    @pl.when(root)
    def _():
        aug[:, :width] = row_p[0, 0]
        identity_beside(aug)
        eliminate(aug, 0, HEAD)

    on_diagonal = jnp.logical_or(root, corner_owner)

    @pl.when(on_diagonal)
    def _():
        pl.semaphore_wait(barrier, rows_n + cols_n - 1)

    @pl.when(jnp.logical_not(on_diagonal))
    def _():
        pl.semaphore_wait(barrier, rows_n + cols_n - 2)

    def send(src, dst, send_sem, recv_sem, device):
        return pltpu.make_async_remote_copy(
            src_ref=src, dst_ref=dst, send_sem=send_sem, recv_sem=recv_sem,
            device_id=device, device_id_type=MESH,
        )

    def corner_copy(which):
        return send(row_p.at[1, 0], corner.at[which], send_t, recv_t.at[which], (0, 0))

    half = cols_n // 2

    def panel_copy(panel, t, slot, target):
        part = row_p.at[panel, t]
        return send(part, part, send_p.at[panel, t, slot], recv_p.at[panel, t], (r, target))

    def panels(panel, t, relay, act):
        targets = [j for j in range(half) if j != panel] + [half + panel]
        if relay:
            targets = [j for j in range(half, cols_n) if j != half + panel]
        for slot, target in enumerate(targets):
            act(panel_copy(panel, t, slot, target))

    chunk = height // CHUNKS

    def chain_copy(which, k, panel):
        part = col_p.at[panel, pl.ds(k * chunk, chunk)]
        target = (sibling, c) if which == 0 else (r + 2, c)
        return send(part, part, send_c.at[which, k], recv_c.at[panel, k], target)

    def spread_copy(phase, step, device):
        buffer = (first, second)[phase]
        return send(buffer, buffer, send_w.at[phase, step], recv_w.at[phase], device)

    pairs = rows_n // 2

    def spread(phase, act):
        @pl.when(root)
        def _():
            for step in range(1, cols_n):
                act(spread_copy(phase, step - 1, (0, step)))

        @pl.when(r == 0)
        def _():
            for step in range(1, pairs):
                act(spread_copy(phase, cols_n - 2 + step, (2 * step, c)))

        @pl.when(parity == 0)
        def _():
            act(spread_copy(phase, cols_n - 2 + pairs, (r + 1, c)))

    def wait_spread(phase):
        @pl.when(jnp.logical_not(root))
        def _():
            spread_copy(phase, 0, (sibling, c)).wait_recv()

    @pl.when(jnp.logical_and(r < 2, c == 1))
    def _():
        for which in range(2):
            @pl.when(r == which)
            def _():
                corner_copy(which).start()

    for panel in range(2):
        @pl.when(c == panel)
        def _():
            for t in range(tiles_r):
                panels(panel, t, False, lambda copy: copy.start())

    def relay(t):
        for panel in range(2):
            @pl.when(c == half + panel)
            def _():
                panel_copy(panel, t, 0, 0).wait_recv()
                panels(panel, t, True, lambda copy: copy.start())

    for k in range(CHUNKS):
        @pl.when(r >= 2)
        def _():
            chain_copy(0, k, parity).wait_recv()

        @pl.when(r + 2 < rows_n)
        def _():
            chain_copy(1, k, parity).start()

        chain_copy(0, k, parity).start()
        if k % PART == 0 and k // PART < tiles_r:
            relay(k // PART)

    def wait_panel(panel):
        @pl.when(jnp.logical_and(c != panel, c != half + panel))
        def _():
            for t in range(tiles_r):
                panel_copy(panel, t, 0, 0).wait_recv()

    @pl.when(root)
    def _():
        eliminate(aug, HEAD, width // (8 * GROUPS))
        first[:width] = aug[:, width:]
        corner_copy(0).wait_recv()
        first[width:] = dot(corner[0], first[:width], ((0,), (1,)))

    wait_spread(0)
    spread(0, lambda copy: copy.start())

    @pl.when(root)
    def _():
        corner_copy(1).wait_recv()
        lower = first[width:]
        aug[:, :width] = corner[1] - dot(lower, lower, NT)
        identity_beside(aug)
        eliminate(aug, 0, width // (8 * GROUPS))
        second[...] = aug[:, width:]
        spread(1, lambda copy: copy.start())

    wait_panel(0)
    wait_panel(1)
    for k in range(CHUNKS):
        chain_copy(0, k, 1 - parity).wait_recv()

    w0 = first[:width]
    lower = first[width:]
    last = [min(tiles_c, ((t + 1) * rows_n - 1) // cols_n + 1) for t in range(tiles_r)]
    for t in range(tiles_r):
        x0 = dot(row_p[0, t], w0, NT)
        x_s[0, t] = x0
        r_s[t] = row_p[1, t] - dot(x0, lower, NT)
    for s in range(tiles_c):
        part = pl.ds(s, width, stride=tiles_c)
        y0 = dot(w0, col_p[0, part, :], NN)
        y_s[0, s] = y0
        y_s[1, s] = col_p[1, part, :] - dot(lower, y0, NN)
    for t in range(tiles_r):
        for s in range(last[t]):
            part = pl.ds(s, width, stride=tiles_c)
            o_ref[t, part, :] = m_ref[t, part, :] - dot(x_s[0, t], y_s[0, s], NN)

    wait_spread(1)

    @pl.when(jnp.logical_not(root))
    def _():
        spread(1, lambda copy: copy.start())

    w1 = second[...]
    for t in range(tiles_r):
        x_s[1, t] = dot(r_s[t], w1, NT)
    for s in range(tiles_c):
        y_s[1, s] = dot(w1, y_s[1, s], NN)
    down = lax.broadcasted_iota(jnp.int32, (width, width), 0)
    across = lax.broadcasted_iota(jnp.int32, (width, width), 1)
    ahead = down - across
    for t in range(tiles_r):
        for s in range(tiles_c):
            part = pl.ds(s, width, stride=tiles_c)
            if s >= last[t]:
                o_ref[t, part, :] = jnp.zeros((width, width), jnp.float32)
                continue
            value = o_ref[t, part, :] - dot(x_s[1, t], y_s[1, s], NN)
            if s == 0:
                value = jnp.where(c == 0, x_s[0, t], jnp.where(c == 1, x_s[1, t], value))
            offset = ((t * rows_n + r) - (s * cols_n + c)) * width
            o_ref[t, part, :] = jnp.where(ahead + offset >= 0, value, 0.0)

    @pl.when(jnp.logical_and(r < 2, c == 1))
    def _():
        corner_copy(0).wait_send()

    for panel in range(2):
        for t in range(tiles_r):
            for owner, passed_on in ((panel, False), (half + panel, True)):
                @pl.when(c == owner)
                def _():
                    panels(panel, t, passed_on, lambda copy: copy.wait_send())

    for k in range(CHUNKS):
        @pl.when(r + 2 < rows_n)
        def _():
            chain_copy(1, k, parity).wait_send()

        chain_copy(0, k, parity).wait_send()
    for phase in range(2):
        spread(phase, lambda copy: copy.wait_send())


def body(matrix, rows_n, cols_n):
    tiles_r, width, tiles_c, _ = matrix.shape
    height = width * tiles_c
    spreads = cols_n - 1 + rows_n // 2
    f32 = jnp.float32
    out = pl.pallas_call(
        functools.partial(kernel, rows_n, cols_n),
        out_shape=jax.ShapeDtypeStruct((tiles_r, height, width), f32),
        in_specs=[pl.BlockSpec(memory_space=pltpu.VMEM)],
        out_specs=pl.BlockSpec(memory_space=pltpu.VMEM),
        scratch_shapes=[
            pltpu.VMEM((2, tiles_r, width, width), f32),
            pltpu.VMEM((2, height, width), f32),
            pltpu.VMEM((2 * width, width), f32),
            pltpu.VMEM((width, width), f32),
            pltpu.VMEM((2, width, width), f32),
            pltpu.VMEM((width, 2 * width), f32),
            pltpu.VMEM((2, tiles_r, width, width), f32),
            pltpu.VMEM((tiles_r, width, width), f32),
            pltpu.VMEM((2, tiles_c, width, width), f32),
            pltpu.SemaphoreType.DMA((2, tiles_r, max(cols_n // 2, 1))),
            pltpu.SemaphoreType.DMA((2, tiles_r)),
            pltpu.SemaphoreType.DMA((2, CHUNKS)),
            pltpu.SemaphoreType.DMA((2, CHUNKS)),
            pltpu.SemaphoreType.DMA((2, spreads)),
            pltpu.SemaphoreType.DMA((2,)),
            pltpu.SemaphoreType.DMA(()),
            pltpu.SemaphoreType.DMA((2,)),
        ],
        compiler_params=pltpu.CompilerParams(
            collective_id=0, has_side_effects=True, vmem_limit_bytes=32 * 1024 * 1024
        ),
    )(matrix.reshape(tiles_r, height, width))
    return out.reshape(matrix.shape)


def solution(mesh):
    placed = P(None, "row", None, "col")
    return jax.shard_map(
        functools.partial(body, rows_n=mesh.shape["row"], cols_n=mesh.shape["col"]),
        mesh=mesh, in_specs=(placed,), out_specs=placed, check_vma=False,
    )
```

```python
import functools

import jax
import jax.numpy as jnp
from jax import lax
from jax.experimental import pallas as pl
from jax.experimental.pallas import tpu as pltpu
from jax.sharding import PartitionSpec as P

MESH = pl.DeviceIdType.MESH
HIGHEST = lax.Precision.HIGHEST
GROUPS = 2
HEAD = 2


def dot(a, b, dims):
    return lax.dot_general(
        a, b, (dims, ((), ())), precision=HIGHEST, preferred_element_type=jnp.float32
    )


NN = ((1,), (0,))
NT = ((1,), (1,))
TN = ((0,), (0,))


def split(x):
    high = x.astype(jnp.bfloat16).astype(jnp.float32)
    rest = x - high
    middle = rest.astype(jnp.bfloat16).astype(jnp.float32)
    return high, middle, rest - middle


def outer_product(a, b):
    a0, a1, a2 = split(a)
    b0, b1, b2 = split(b)
    left = jnp.concatenate([a0, a0, a1, a0, a2, a1], 0).astype(jnp.bfloat16)
    right = jnp.concatenate([b0, b1, b0, b2, b0, b1], 0).astype(jnp.bfloat16)
    return lax.dot_general(left, right, (TN, ((), ())), preferred_element_type=jnp.float32)


def identity_beside(aug):
    n = aug.shape[0]
    rows = lax.broadcasted_iota(jnp.int32, (n, n), 0)
    lanes = lax.broadcasted_iota(jnp.int32, (n, n), 1)
    aug[:, n:] = jnp.where(rows == lanes, 1.0, 0.0)


def eliminate(aug, first, last):
    n = aug.shape[0]
    sub = lax.broadcasted_iota(jnp.int32, (8, n), 0)
    lane = lax.broadcasted_iota(jnp.int32, (8 * GROUPS, n), 1)
    block = 8 * GROUPS

    def spread_row(x, i):
        return jnp.broadcast_to(x[i : i + 1], (8, n))

    for b in range(first, last):
        base = b * block
        left = [aug[base + 8 * g : base + 8 * g + 8, :n] for g in range(GROUPS)]
        right = [aug[base + 8 * g : base + 8 * g + 8, n:] for g in range(GROUPS)]
        cols = [
            [jnp.broadcast_to(left[g][:, base + k : base + k + 1], (8, n)) for k in range(8 * g + 8)]
            for g in range(GROUPS)
        ]
        scale = [jnp.zeros((8, n), jnp.float32) for _ in range(GROUPS)]
        for k in range(block):
            own, row = divmod(k, 8)
            inverse = lax.rsqrt(spread_row(cols[own][k], row))
            scale[own] = jnp.where(sub == row, inverse, scale[own])
            if k == block - 1:
                break
            factor = {g: cols[g][k] * inverse for g in range(own, GROUPS)}
            row_left = spread_row(left[own], row) * inverse
            row_right = spread_row(right[own], row) * inverse
            pivots = {j: spread_row(factor[j // 8], j % 8) for j in range(k + 1, block)}
            for g in range(own, GROUPS):
                if g == own and row == 7:
                    continue
                for j in range(k + 1, 8 * g + 8):
                    cols[g][j] = cols[g][j] - factor[g] * pivots[j]
                below = jnp.where(sub > row, factor[g], 0.0) if g == own else factor[g]
                left[g] = left[g] - below * row_left
                right[g] = right[g] - below * row_right
        done_right = jnp.concatenate([right[g] * scale[g] for g in range(GROUPS)], 0)
        if base + block < n:
            done_left = jnp.concatenate([left[g] * scale[g] for g in range(GROUPS)], 0)
            later = jnp.where(lane >= base + block, done_left, 0.0)
            change = outer_product(later, jnp.concatenate([done_left, done_right], 1))
            aug[base + block :] -= change[base + block :]
        aug[base : base + block, n:] = done_right


def kernel(
    rows_n, cols_n, m_ref, o_ref, row_p, col_p, first, second, corner, aug, x_s, r_s, y_s,
    send_p, recv_p, send_c, recv_c, send_w, recv_w, send_t, recv_t,
):
    r = lax.axis_index("row")
    c = lax.axis_index("col")
    tiles_r, height, width = m_ref.shape
    tiles_c = height // width
    parity = lax.rem(r, 2)
    sibling = r + 1 - 2 * parity
    root = jnp.logical_and(r == 0, c == 0)
    corner_owner = jnp.logical_and(r == 1, c == 1)

    barrier = pltpu.get_barrier_semaphore()
    for step in range(1, cols_n):
        pl.semaphore_signal(
            barrier, inc=1, device_id=(r, lax.rem(c + step, cols_n)), device_id_type=MESH
        )
    for step in range(1, rows_n):
        pl.semaphore_signal(
            barrier, inc=1, device_id=(lax.rem(r + step, rows_n), c), device_id_type=MESH
        )

    @pl.when(jnp.logical_or(root, corner_owner))
    def _():
        pl.semaphore_signal(barrier, inc=1, device_id=(1 - r, 1 - c), device_id_type=MESH)

    @pl.when(c < 2)
    def _():
        for t in range(tiles_r):
            row_p[c, t] = m_ref[t, pl.ds(0, width, stride=tiles_c), :]

    @pl.when(r < 2)
    def _():
        for s in range(tiles_c):
            col_p[parity, s] = m_ref[0, pl.ds(s, width, stride=tiles_c), :]

    @pl.when(root)
    def _():
        aug[:, :width] = row_p[0, 0]
        identity_beside(aug)
        eliminate(aug, 0, HEAD)

    on_diagonal = jnp.logical_or(root, corner_owner)

    @pl.when(on_diagonal)
    def _():
        pl.semaphore_wait(barrier, rows_n + cols_n - 1)

    @pl.when(jnp.logical_not(on_diagonal))
    def _():
        pl.semaphore_wait(barrier, rows_n + cols_n - 2)

    def send(src, dst, send_sem, recv_sem, device):
        return pltpu.make_async_remote_copy(
            src_ref=src, dst_ref=dst, send_sem=send_sem, recv_sem=recv_sem,
            device_id=device, device_id_type=MESH,
        )

    def corner_copy(which):
        return send(row_p.at[1, 0], corner.at[which], send_t, recv_t.at[which], (0, 0))

    half = cols_n // 2

    def panel_copy(panel, t, slot, target):
        part = row_p.at[panel, t]
        return send(part, part, send_p.at[panel, t, slot], recv_p.at[panel, t], (r, target))

    def panels(panel, t, relay, act):
        targets = [j for j in range(half) if j != panel] + [half + panel]
        if relay:
            targets = [j for j in range(half, cols_n) if j != half + panel]
        for slot, target in enumerate(targets):
            act(panel_copy(panel, t, slot, target))

    def chain_copy(which, k, panel):
        part = col_p.at[panel, k]
        target = (sibling, c) if which == 0 else (r + 2, c)
        return send(part, part, send_c.at[which, k], recv_c.at[panel, k], target)

    def spread_copy(phase, step, device):
        buffer = (first, second)[phase]
        return send(buffer, buffer, send_w.at[phase, step], recv_w.at[phase], device)

    pairs = rows_n // 2

    def spread(phase, act):
        @pl.when(root)
        def _():
            for step in range(1, cols_n):
                act(spread_copy(phase, step - 1, (0, step)))

        @pl.when(r == 0)
        def _():
            for step in range(1, pairs):
                act(spread_copy(phase, cols_n - 2 + step, (2 * step, c)))

        @pl.when(parity == 0)
        def _():
            act(spread_copy(phase, cols_n - 2 + pairs, (r + 1, c)))

    def wait_spread(phase):
        @pl.when(jnp.logical_not(root))
        def _():
            spread_copy(phase, 0, (sibling, c)).wait_recv()

    @pl.when(jnp.logical_and(r < 2, c == 1))
    def _():
        for which in range(2):
            @pl.when(r == which)
            def _():
                corner_copy(which).start()

    for panel in range(2):
        @pl.when(c == panel)
        def _():
            for t in range(tiles_r):
                panels(panel, t, False, lambda copy: copy.start())

    def relay(t):
        for panel in range(2):
            @pl.when(c == half + panel)
            def _():
                panel_copy(panel, t, 0, 0).wait_recv()
                panels(panel, t, True, lambda copy: copy.start())

    def pass_on(k):
        @pl.when(r >= 2)
        def _():
            chain_copy(0, k, parity).wait_recv()

        @pl.when(r + 2 < rows_n)
        def _():
            chain_copy(1, k, parity).start()

        chain_copy(0, k, parity).start()
    ahead_by = max(tiles_c // 2, 1)
    for k in range(max(ahead_by, tiles_r)):
        if k < tiles_r:
            relay(k)
        if k < ahead_by:
            pass_on(k)

    def wait_panel(panel):
        @pl.when(jnp.logical_and(c != panel, c != half + panel))
        def _():
            for t in range(tiles_r):
                panel_copy(panel, t, 0, 0).wait_recv()

    @pl.when(r < 2)
    def _():
        for k in range(ahead_by, tiles_c):
            pass_on(k)

    @pl.when(root)
    def _():
        eliminate(aug, HEAD, width // (8 * GROUPS))
        first[:width] = aug[:, width:]
        corner_copy(0).wait_recv()
        first[width:] = dot(corner[0], first[:width], ((0,), (1,)))

    wait_spread(0)
    spread(0, lambda copy: copy.start())

    @pl.when(root)
    def _():
        corner_copy(1).wait_recv()
        lower = first[width:]
        aug[:, :width] = corner[1] - dot(lower, lower, NT)
        identity_beside(aug)
        eliminate(aug, 0, width // (8 * GROUPS))
        second[...] = aug[:, width:]
        spread(1, lambda copy: copy.start())

    wait_panel(0)
    wait_panel(1)
    w0 = first[:width]
    lower = first[width:]
    last = [min(tiles_c, ((t + 1) * rows_n - 1) // cols_n + 1) for t in range(tiles_r)]
    for t in range(tiles_r):
        x0 = dot(row_p[0, t], w0, NT)
        x_s[0, t] = x0
        r_s[t] = row_p[1, t] - dot(x0, lower, NT)
    for s in range(tiles_c):
        if s + ahead_by < tiles_c:
            @pl.when(r >= 2)
            def _():
                pass_on(s + ahead_by)

        chain_copy(0, s, 1 - parity).wait_recv()
        part = pl.ds(s, width, stride=tiles_c)
        y0 = dot(w0, col_p[0, s], NN)
        y_s[0, s] = y0
        y_s[1, s] = col_p[1, s] - dot(lower, y0, NN)
        for t in range(tiles_r):
            if s < last[t]:
                o_ref[t, part, :] = m_ref[t, part, :] - dot(x_s[0, t], y0, NN)

    wait_spread(1)

    @pl.when(jnp.logical_not(root))
    def _():
        spread(1, lambda copy: copy.start())

    w1 = second[...]
    for t in range(tiles_r):
        x_s[1, t] = dot(r_s[t], w1, NT)
    for s in range(tiles_c):
        y_s[1, s] = dot(w1, y_s[1, s], NN)
    down = lax.broadcasted_iota(jnp.int32, (width, width), 0)
    across = lax.broadcasted_iota(jnp.int32, (width, width), 1)
    ahead = down - across
    for t in range(tiles_r):
        for s in range(tiles_c):
            part = pl.ds(s, width, stride=tiles_c)
            if s >= last[t]:
                o_ref[t, part, :] = jnp.zeros((width, width), jnp.float32)
                continue
            value = o_ref[t, part, :] - dot(x_s[1, t], y_s[1, s], NN)
            if s == 0:
                value = jnp.where(c == 0, x_s[0, t], jnp.where(c == 1, x_s[1, t], value))
            offset = ((t * rows_n + r) - (s * cols_n + c)) * width
            o_ref[t, part, :] = jnp.where(ahead + offset >= 0, value, 0.0)

    @pl.when(jnp.logical_and(r < 2, c == 1))
    def _():
        corner_copy(0).wait_send()

    for panel in range(2):
        for t in range(tiles_r):
            for owner, passed_on in ((panel, False), (half + panel, True)):
                @pl.when(c == owner)
                def _():
                    panels(panel, t, passed_on, lambda copy: copy.wait_send())

    for k in range(tiles_c):
        @pl.when(r + 2 < rows_n)
        def _():
            chain_copy(1, k, parity).wait_send()

        chain_copy(0, k, parity).wait_send()
    for phase in range(2):
        spread(phase, lambda copy: copy.wait_send())


def body(matrix, rows_n, cols_n):
    tiles_r, width, tiles_c, _ = matrix.shape
    height = width * tiles_c
    spreads = cols_n - 1 + rows_n // 2
    f32 = jnp.float32
    out = pl.pallas_call(
        functools.partial(kernel, rows_n, cols_n),
        out_shape=jax.ShapeDtypeStruct((tiles_r, height, width), f32),
        in_specs=[pl.BlockSpec(memory_space=pltpu.VMEM)],
        out_specs=pl.BlockSpec(memory_space=pltpu.VMEM),
        scratch_shapes=[
            pltpu.VMEM((2, tiles_r, width, width), f32),
            pltpu.VMEM((2, tiles_c, width, width), f32),
            pltpu.VMEM((2 * width, width), f32),
            pltpu.VMEM((width, width), f32),
            pltpu.VMEM((2, width, width), f32),
            pltpu.VMEM((width, 2 * width), f32),
            pltpu.VMEM((2, tiles_r, width, width), f32),
            pltpu.VMEM((tiles_r, width, width), f32),
            pltpu.VMEM((2, tiles_c, width, width), f32),
            pltpu.SemaphoreType.DMA((2, tiles_r, max(cols_n // 2, 1))),
            pltpu.SemaphoreType.DMA((2, tiles_r)),
            pltpu.SemaphoreType.DMA((2, tiles_c)),
            pltpu.SemaphoreType.DMA((2, tiles_c)),
            pltpu.SemaphoreType.DMA((2, spreads)),
            pltpu.SemaphoreType.DMA((2,)),
            pltpu.SemaphoreType.DMA(()),
            pltpu.SemaphoreType.DMA((2,)),
        ],
        compiler_params=pltpu.CompilerParams(
            collective_id=0, has_side_effects=True, vmem_limit_bytes=32 * 1024 * 1024
        ),
    )(matrix.reshape(tiles_r, height, width))
    return out.reshape(matrix.shape)


def solution(mesh):
    placed = P(None, "row", None, "col")
    return jax.shard_map(
        functools.partial(body, rows_n=mesh.shape["row"], cols_n=mesh.shape["col"]),
        mesh=mesh, in_specs=(placed,), out_specs=placed, check_vma=False,
    )
```

```python
import functools

import jax
import jax.numpy as jnp
from jax import lax
from jax.experimental import pallas as pl
from jax.experimental.pallas import tpu as pltpu
from jax.sharding import PartitionSpec as P

MESH = pl.DeviceIdType.MESH
HIGHEST = lax.Precision.HIGHEST
GROUPS = 2
HEAD = 2


def dot(a, b, dims):
    return lax.dot_general(
        a, b, (dims, ((), ())), precision=HIGHEST, preferred_element_type=jnp.float32
    )


def product(a, b):
    a0 = a.astype(jnp.bfloat16)
    a1 = (a - a0.astype(jnp.float32)).astype(jnp.bfloat16)
    b0 = b.astype(jnp.bfloat16)
    b1 = (b - b0.astype(jnp.float32)).astype(jnp.bfloat16)
    left = jnp.concatenate([a0, a0, a1], 1)
    right = jnp.concatenate([b0, b1, b0], 0)
    return lax.dot_general(left, right, (NN, ((), ())), preferred_element_type=jnp.float32)


NN = ((1,), (0,))
NT = ((1,), (1,))
TN = ((0,), (0,))


def split(x):
    high = x.astype(jnp.bfloat16).astype(jnp.float32)
    rest = x - high
    middle = rest.astype(jnp.bfloat16).astype(jnp.float32)
    return high, middle, rest - middle


def outer_product(a, b):
    a0, a1, a2 = split(a)
    b0, b1, b2 = split(b)
    left = jnp.concatenate([a0, a0, a1, a0, a2, a1], 0).astype(jnp.bfloat16)
    right = jnp.concatenate([b0, b1, b0, b2, b0, b1], 0).astype(jnp.bfloat16)
    return lax.dot_general(left, right, (TN, ((), ())), preferred_element_type=jnp.float32)


def identity_beside(aug):
    n = aug.shape[0]
    rows = lax.broadcasted_iota(jnp.int32, (n, n), 0)
    lanes = lax.broadcasted_iota(jnp.int32, (n, n), 1)
    aug[:, n:] = jnp.where(rows == lanes, 1.0, 0.0)


def eliminate(aug, first, last):
    n = aug.shape[0]
    sub = lax.broadcasted_iota(jnp.int32, (8, n), 0)
    lane = lax.broadcasted_iota(jnp.int32, (8 * GROUPS, n), 1)
    block = 8 * GROUPS

    def spread_row(x, i):
        return jnp.broadcast_to(x[i : i + 1], (8, n))

    for b in range(first, last):
        base = b * block
        left = [aug[base + 8 * g : base + 8 * g + 8, :n] for g in range(GROUPS)]
        right = [aug[base + 8 * g : base + 8 * g + 8, n:] for g in range(GROUPS)]
        cols = [
            [jnp.broadcast_to(left[g][:, base + k : base + k + 1], (8, n)) for k in range(8 * g + 8)]
            for g in range(GROUPS)
        ]
        scale = [jnp.zeros((8, n), jnp.float32) for _ in range(GROUPS)]
        for k in range(block):
            own, row = divmod(k, 8)
            inverse = lax.rsqrt(spread_row(cols[own][k], row))
            scale[own] = jnp.where(sub == row, inverse, scale[own])
            if k == block - 1:
                break
            factor = {g: cols[g][k] * inverse for g in range(own, GROUPS)}
            row_left = spread_row(left[own], row) * inverse
            row_right = spread_row(right[own], row) * inverse
            pivots = {j: spread_row(factor[j // 8], j % 8) for j in range(k + 1, block)}
            for g in range(own, GROUPS):
                if g == own and row == 7:
                    continue
                for j in range(k + 1, 8 * g + 8):
                    cols[g][j] = cols[g][j] - factor[g] * pivots[j]
                below = jnp.where(sub > row, factor[g], 0.0) if g == own else factor[g]
                left[g] = left[g] - below * row_left
                right[g] = right[g] - below * row_right
        done_right = jnp.concatenate([right[g] * scale[g] for g in range(GROUPS)], 0)
        if base + block < n:
            done_left = jnp.concatenate([left[g] * scale[g] for g in range(GROUPS)], 0)
            later = jnp.where(lane >= base + block, done_left, 0.0)
            change = outer_product(later, jnp.concatenate([done_left, done_right], 1))
            aug[base + block :] -= change[base + block :]
        aug[base : base + block, n:] = done_right


def kernel(
    rows_n, cols_n, m_ref, o_ref, row_p, col_p, first, second, corner, aug, x_s, r_s, y_s,
    send_p, recv_p, send_c, recv_c, send_w, recv_w, send_t, recv_t,
):
    r = lax.axis_index("row")
    c = lax.axis_index("col")
    tiles_r, height, width = m_ref.shape
    tiles_c = height // width
    parity = lax.rem(r, 2)
    sibling = r + 1 - 2 * parity
    root = jnp.logical_and(r == 0, c == 0)
    corner_owner = jnp.logical_and(r == 1, c == 1)

    barrier = pltpu.get_barrier_semaphore()
    for step in range(1, cols_n):
        pl.semaphore_signal(
            barrier, inc=1, device_id=(r, lax.rem(c + step, cols_n)), device_id_type=MESH
        )
    for step in range(1, rows_n):
        pl.semaphore_signal(
            barrier, inc=1, device_id=(lax.rem(r + step, rows_n), c), device_id_type=MESH
        )

    @pl.when(jnp.logical_or(root, corner_owner))
    def _():
        pl.semaphore_signal(barrier, inc=1, device_id=(1 - r, 1 - c), device_id_type=MESH)

    @pl.when(c < 2)
    def _():
        for t in range(tiles_r):
            row_p[c, t] = m_ref[t, pl.ds(0, width, stride=tiles_c), :]

    @pl.when(r < 2)
    def _():
        for s in range(tiles_c):
            col_p[parity, s] = m_ref[0, pl.ds(s, width, stride=tiles_c), :]

    @pl.when(root)
    def _():
        aug[:, :width] = row_p[0, 0]
        identity_beside(aug)
        eliminate(aug, 0, HEAD)

    on_diagonal = jnp.logical_or(root, corner_owner)

    @pl.when(on_diagonal)
    def _():
        pl.semaphore_wait(barrier, rows_n + cols_n - 1)

    @pl.when(jnp.logical_not(on_diagonal))
    def _():
        pl.semaphore_wait(barrier, rows_n + cols_n - 2)

    def send(src, dst, send_sem, recv_sem, device):
        return pltpu.make_async_remote_copy(
            src_ref=src, dst_ref=dst, send_sem=send_sem, recv_sem=recv_sem,
            device_id=device, device_id_type=MESH,
        )

    def corner_copy(which):
        return send(row_p.at[1, 0], corner.at[which], send_t, recv_t.at[which], (0, 0))

    half = cols_n // 2

    def panel_copy(panel, t, slot, target):
        part = row_p.at[panel, t]
        return send(part, part, send_p.at[panel, t, slot], recv_p.at[panel, t], (r, target))

    def panels(panel, t, relay, act):
        targets = [j for j in range(half) if j != panel] + [half + panel]
        if relay:
            targets = [j for j in range(half, cols_n) if j != half + panel]
        for slot, target in enumerate(targets):
            act(panel_copy(panel, t, slot, target))

    def chain_copy(which, k, panel):
        part = col_p.at[panel, k]
        target = (sibling, c) if which == 0 else (r + 2, c)
        return send(part, part, send_c.at[which, k], recv_c.at[panel, k], target)

    def spread_copy(phase, step, device):
        buffer = (first, second)[phase]
        return send(buffer, buffer, send_w.at[phase, step], recv_w.at[phase], device)

    pairs = rows_n // 2

    def spread(phase, act):
        @pl.when(root)
        def _():
            for step in range(1, cols_n):
                act(spread_copy(phase, step - 1, (0, step)))

        @pl.when(r == 0)
        def _():
            for step in range(1, pairs):
                act(spread_copy(phase, cols_n - 2 + step, (2 * step, c)))

        @pl.when(parity == 0)
        def _():
            act(spread_copy(phase, cols_n - 2 + pairs, (r + 1, c)))

    def wait_spread(phase):
        @pl.when(jnp.logical_not(root))
        def _():
            spread_copy(phase, 0, (sibling, c)).wait_recv()

    @pl.when(jnp.logical_and(r < 2, c == 1))
    def _():
        for which in range(2):
            @pl.when(r == which)
            def _():
                corner_copy(which).start()

    for panel in range(2):
        @pl.when(c == panel)
        def _():
            for t in range(tiles_r):
                panels(panel, t, False, lambda copy: copy.start())

    def relay(t):
        for panel in range(2):
            @pl.when(c == half + panel)
            def _():
                panel_copy(panel, t, 0, 0).wait_recv()
                panels(panel, t, True, lambda copy: copy.start())

    def pass_on(k):
        @pl.when(r >= 2)
        def _():
            chain_copy(0, k, parity).wait_recv()

        @pl.when(r + 2 < rows_n)
        def _():
            chain_copy(1, k, parity).start()

        chain_copy(0, k, parity).start()
    for k in range(max(tiles_c, tiles_r)):
        if k < tiles_c:
            pass_on(k)
        if k < tiles_r:
            relay(k)

    def wait_panel(panel):
        @pl.when(jnp.logical_and(c != panel, c != half + panel))
        def _():
            for t in range(tiles_r):
                panel_copy(panel, t, 0, 0).wait_recv()

    @pl.when(root)
    def _():
        eliminate(aug, HEAD, width // (8 * GROUPS))
        first[:width] = aug[:, width:]
        corner_copy(0).wait_recv()
        first[width:] = dot(corner[0], first[:width], ((0,), (1,)))

    wait_spread(0)
    spread(0, lambda copy: copy.start())

    @pl.when(root)
    def _():
        corner_copy(1).wait_recv()
        lower = first[width:]
        aug[:, :width] = corner[1] - dot(lower, lower, NT)
        identity_beside(aug)
        eliminate(aug, 0, width // (8 * GROUPS))
        second[...] = aug[:, width:]
        spread(1, lambda copy: copy.start())

    wait_panel(0)
    wait_panel(1)
    w0 = first[:width]
    lower = first[width:]
    last = [min(tiles_c, ((t + 1) * rows_n - 1) // cols_n + 1) for t in range(tiles_r)]
    for t in range(tiles_r):
        x0 = dot(row_p[0, t], w0, NT)
        x_s[0, t] = x0
        r_s[t] = row_p[1, t] - dot(x0, lower, NT)
    for s in range(tiles_c):
        chain_copy(0, s, 1 - parity).wait_recv()
        part = pl.ds(s, width, stride=tiles_c)
        y0 = dot(w0, col_p[0, s], NN)
        y_s[0, s] = y0
        y_s[1, s] = col_p[1, s] - dot(lower, y0, NN)
        for t in range(tiles_r):
            if s < last[t]:
                o_ref[t, part, :] = m_ref[t, part, :] - product(x_s[0, t], y0)

    wait_spread(1)

    @pl.when(jnp.logical_not(root))
    def _():
        spread(1, lambda copy: copy.start())

    w1 = second[...]
    for t in range(tiles_r):
        x_s[1, t] = dot(r_s[t], w1, NT)
    for s in range(tiles_c):
        y_s[1, s] = dot(w1, y_s[1, s], NN)
    down = lax.broadcasted_iota(jnp.int32, (width, width), 0)
    across = lax.broadcasted_iota(jnp.int32, (width, width), 1)
    ahead = down - across
    for t in range(tiles_r):
        for s in range(tiles_c):
            part = pl.ds(s, width, stride=tiles_c)
            if s >= last[t]:
                o_ref[t, part, :] = jnp.zeros((width, width), jnp.float32)
                continue
            value = o_ref[t, part, :] - product(x_s[1, t], y_s[1, s])
            if s == 0:
                value = jnp.where(c == 0, x_s[0, t], jnp.where(c == 1, x_s[1, t], value))
            offset = ((t * rows_n + r) - (s * cols_n + c)) * width
            o_ref[t, part, :] = jnp.where(ahead + offset >= 0, value, 0.0)

    @pl.when(jnp.logical_and(r < 2, c == 1))
    def _():
        corner_copy(0).wait_send()

    for panel in range(2):
        for t in range(tiles_r):
            for owner, passed_on in ((panel, False), (half + panel, True)):
                @pl.when(c == owner)
                def _():
                    panels(panel, t, passed_on, lambda copy: copy.wait_send())

    for k in range(tiles_c):
        @pl.when(r + 2 < rows_n)
        def _():
            chain_copy(1, k, parity).wait_send()

        chain_copy(0, k, parity).wait_send()
    for phase in range(2):
        spread(phase, lambda copy: copy.wait_send())


def body(matrix, rows_n, cols_n):
    tiles_r, width, tiles_c, _ = matrix.shape
    height = width * tiles_c
    spreads = cols_n - 1 + rows_n // 2
    f32 = jnp.float32
    out = pl.pallas_call(
        functools.partial(kernel, rows_n, cols_n),
        out_shape=jax.ShapeDtypeStruct((tiles_r, height, width), f32),
        in_specs=[pl.BlockSpec(memory_space=pltpu.VMEM)],
        out_specs=pl.BlockSpec(memory_space=pltpu.VMEM),
        scratch_shapes=[
            pltpu.VMEM((2, tiles_r, width, width), f32),
            pltpu.VMEM((2, tiles_c, width, width), f32),
            pltpu.VMEM((2 * width, width), f32),
            pltpu.VMEM((width, width), f32),
            pltpu.VMEM((2, width, width), f32),
            pltpu.VMEM((width, 2 * width), f32),
            pltpu.VMEM((2, tiles_r, width, width), f32),
            pltpu.VMEM((tiles_r, width, width), f32),
            pltpu.VMEM((2, tiles_c, width, width), f32),
            pltpu.SemaphoreType.DMA((2, tiles_r, max(cols_n // 2, 1))),
            pltpu.SemaphoreType.DMA((2, tiles_r)),
            pltpu.SemaphoreType.DMA((2, tiles_c)),
            pltpu.SemaphoreType.DMA((2, tiles_c)),
            pltpu.SemaphoreType.DMA((2, spreads)),
            pltpu.SemaphoreType.DMA((2,)),
            pltpu.SemaphoreType.DMA(()),
            pltpu.SemaphoreType.DMA((2,)),
        ],
        compiler_params=pltpu.CompilerParams(
            collective_id=0, has_side_effects=True, vmem_limit_bytes=32 * 1024 * 1024
        ),
    )(matrix.reshape(tiles_r, height, width))
    return out.reshape(matrix.shape)


def solution(mesh):
    placed = P(None, "row", None, "col")
    return jax.shard_map(
        functools.partial(body, rows_n=mesh.shape["row"], cols_n=mesh.shape["col"]),
        mesh=mesh, in_specs=(placed,), out_specs=placed, check_vma=False,
    )
```
